32 devices in a mesh: fsdp: 4 (over y, x), expert: 2 (over core), tensor: 4 (over z).
Axes of the slice: x: 2, y: 2, z: 4, core: 2. Of those that a mesh axis runs over, the one named last changes fastest.
Arguments:
- tokens: bfloat16 [6304, 768], P(('fsdp', 'expert')), may hold values from -6 to 6
- routes: int32 [6304, 2], P(('fsdp', 'expert')), may hold values from 0 to 7, all different within a row; in each aligned block of 788 rows (0 to 787, 788 to 1575, ...) at most 296 rows name the same one
- cotangent: bfloat16 [6304, 768], P(('fsdp', 'expert')), may hold values from -6 to 6
- ln_gain: bfloat16 [2, 2, 768], P(None, None, 'fsdp'), may hold values from 0.5 to 1.5
- ln_bias: bfloat16 [2, 2, 768], P(None, None, 'fsdp'), may hold values from -3 to 3
- w_qkv: bfloat16 [2, 768, 3, 768], P(None, 'fsdp', None, 'tensor'), may hold values from -0.21875 to 0.21875
- w_out: bfloat16 [2, 768, 768], P(None, 'tensor', 'fsdp'), may hold values from -1.5 to 1.5
- w_router: bfloat16 [2, 768, 8], P(None, 'fsdp'), may hold values from -0.15625 to 0.15625
- w_in: bfloat16 [2, 8, 768, 3072], P(None, ('fsdp', 'expert'), None, 'tensor'), may hold values from -0.21875 to 0.21875
- w_back: bfloat16 [2, 8, 3072, 768], P(None, ('fsdp', 'expert'), 'tensor'), may hold values from -1 to 1
Outputs:
- output: bfloat16 [6304, 768], P(('fsdp', 'expert'))
- grad_tokens: float32 [6304, 768], P(('fsdp', 'expert'))
- grad_ln_gain: float32 [2, 2, 768], P(None, None, 'fsdp')
- grad_ln_bias: float32 [2, 2, 768], P(None, None, 'fsdp')
- grad_qkv: float32 [2, 768, 3, 768], P(None, 'fsdp', None, 'tensor')
- grad_out: float32 [2, 768, 768], P(None, 'tensor', 'fsdp')
- grad_router: float32 [2, 768, 8], P(None, 'fsdp')
- grad_in: float32 [2, 8, 768, 3072], P(None, ('fsdp', 'expert'), None, 'tensor')
- grad_back: float32 [2, 8, 3072, 768], P(None, ('fsdp', 'expert'), 'tensor')
The draws below stay inside these ranges and needn't reach their ends.
Inputs may be any that keep to these rules, and one draw needn't show every extreme that they name: `routes`: each row names 2 different experts. In the rows of one index of fsdp and expert (aligned blocks of 788 rows) no expert is named more than 296 times, a bound that some block reaches.
All inputs are finite; a program needn't handle non-finite values.
Results may differ from the reference program's by a relative error of at most 0.02.
Values may be sent and summed in bfloat16 or wider, within the bound.
A program may use at most 192 MiB of HBM per device.

```python
import math
import jax
import jax.numpy as jnp
import numpy as np
from jax import lax

D = 768
HEADS = 12
HEAD_DIM = 64
FF = 3072
SEQ = 197
LAYERS = 2
TOP = 2
EXPERTS = 8
TOK_DEV = 788
IMAGES = 32
TOKENS = 6304
CAP = 296
N_FSDP = 4
N_EXPERT = 2


def block_levels(own_key, shape, pieces, least, top_value):
    def one(position, parts):
        heights = jax.random.uniform(jax.random.fold_in(jax.random.fold_in(own_key, 6), position), (parts,), jnp.float32, least / len(pieces), top_value / len(pieces))
        return jnp.repeat(jnp.exp(heights), shape[position] // parts).reshape((-1,) + (1,) * (len(shape) - position - 1))

    loudness = one(*pieces[0])
    for cut in pieces[1:]:
        loudness = loudness * one(*cut)
    return loudness


def routed_block(rng, own, number, rows, count, top, reach, slope):
    sequence = jax.random.permutation(rng, count)
    crowded, usual = shares(count, rows * top, reach, slope, True), shares(count, rows * top, reach, slope, False)
    places = jnp.arange(count)

    def named(sizes, offset_by):
        used = int((sizes > 0).sum())
        fixed = max(1, used // 4)
        passed = fixed + (places - fixed + offset_by * (used - fixed)) % max(1, count - fixed)
        return jnp.zeros((count,), jnp.int32).at[sequence[jnp.where(places < fixed, places, passed)]].set(jnp.asarray(sizes, jnp.int32))

    sizes = jnp.where(number % 4 == 0, named(crowded, number // 4), named(usual, number - number // 4 - 1))
    mixed = jax.random.permutation(jax.random.fold_in(own, 3), count)
    donor, receiver = mixed[0:count // 2 * 2:2], mixed[1:count // 2 * 2:2]
    margin = jnp.minimum(sizes[donor] - 1, reach - sizes[receiver]) // 2
    margin = jnp.where((donor == sequence[0]) | (receiver == sequence[0]) | (sizes[receiver] == 0), 0, jnp.maximum(margin, 0))
    passed = jax.random.randint(jax.random.fold_in(own, 4), (count // 2,), 0, 1 << 20) % (margin + 1)
    sizes = sizes.at[donor].add(-passed).at[receiver].add(passed)
    items = jnp.searchsorted(jnp.cumsum(sizes), jnp.arange(rows * top), side="right").astype(jnp.int32)
    grid = items.reshape(top, rows).T
    grid = grid[jax.random.permutation(jax.random.fold_in(own, 1), rows)]
    offset_by = jax.random.randint(jax.random.fold_in(own, 2), (rows, 1), 0, top)
    return jnp.take_along_axis(grid, (jnp.arange(top)[None, :] + offset_by) % top, axis=1)


def shares(count, total, bound, skew, full):
    loads = [(1 << 20) // math.isqrt(rank ** skew) + 1 for rank in range(1, count + 1)]
    largest = bound if full else min(bound, max(-(-total // count), total * loads[0] // sum(loads)))
    least = 1 if total - largest >= count - 1 else 0
    given, spare = [largest] + [least] * (count - 1), total - largest - least * (count - 1)
    while spare > 0:
        candidates = [i for i in range(1, count) if given[i] < largest] or [i for i in range(1, count) if given[i] < bound]
        pool, remaining = sum([loads[i] for i in candidates]), spare
        for i in candidates:
            addition = min(bound - given[i], max(1, remaining * loads[i] // pool), spare)
            given[i] = given[i] + addition
            spare = spare - addition
    return np.array(given)


def bell_draw(stream_key, shape, width, most, cuts=(), kind=jnp.bfloat16):
    gain = block_levels(stream_key, shape, cuts, -0.22, 0.18) if cuts else 1.0
    array = jax.random.normal(stream_key, shape, jnp.float32) * width * gain
    return jnp.minimum(jnp.maximum(array, -most), most).astype(kind)


def setup_inputs(seed: int = 0) -> dict:
    keys = jax.random.split(jax.random.key(seed), 11)
    tokens = bell_draw(keys[0], (TOKENS, D), 1.0, 6.0, ((0, 8),))
    routes_keys = jax.random.split(jax.random.fold_in(keys[1], 1), TOKENS // TOK_DEV)
    routes_turns = jax.random.permutation(jax.random.fold_in(keys[1], 3), TOKENS // TOK_DEV)
    routes = jax.vmap(lambda own, number: routed_block(jax.random.fold_in(keys[1], 2), own, number, TOK_DEV, EXPERTS, TOP, CAP, 2))(routes_keys, routes_turns).reshape((TOKENS, TOP))
    cotangent = bell_draw(keys[2], (TOKENS, D), 1.0, 6.0, ((0, 8),))
    ln_gain = jnp.clip(1.0 + 0.1 * jax.random.normal(keys[3], (LAYERS, 2, D), jnp.float32), 0.5, 1.5).astype(jnp.bfloat16)
    ln_bias = bell_draw(keys[4], (LAYERS, 2, D), 0.5, 3.0, ((2, 4),))
    w_qkv = bell_draw(keys[5], (LAYERS, D, 3, D), D ** -0.5, 0.21875, ((1, 4), (3, 4)))
    w_out = bell_draw(keys[6], (LAYERS, D, D), (D // 48) ** -0.5, 1.5, ((1, 4), (2, 4)))
    w_router = bell_draw(keys[7], (LAYERS, D, EXPERTS), (2 * D) ** -0.5, 0.15625, ((1, 4),))
    w_in = bell_draw(keys[8], (LAYERS, EXPERTS, D, FF), D ** -0.5, 0.21875, ((1, 8), (3, 4)))
    w_back = bell_draw(keys[9], (LAYERS, EXPERTS, FF, D), (max(FF * 3 // (4 * EXPERTS * EXPERTS), 1)) ** -0.5, 1.0, ((1, 8), (2, 4)))
    return {"tokens": tokens, "routes": routes, "cotangent": cotangent, "ln_gain": ln_gain, "ln_bias": ln_bias, "w_qkv": w_qkv, "w_out": w_out, "w_router": w_router, "w_in": w_in, "w_back": w_back}


@jax.custom_vjp
def low(v):
    return lax.optimization_barrier(v.astype(jnp.bfloat16)).astype(jnp.float32)

@jax.custom_vjp
def low_back(v):
    return v

def low_keep(v):
    return (low(v), None)

def low_pass(kept, grad):
    return (grad,)

def back_keep(v):
    return (v, None)

def back_low(kept, grad):
    return (low(grad),)
low.defvjp(low_keep, low_pass)
low_back.defvjp(back_keep, back_low)
highest = lax.Precision.HIGHEST
epsilon = 1e-06

def layer_norm(values, gain_row, bias_row):
    center = values - lax.optimization_barrier(jnp.mean(values, axis=-1, keepdims=True))
    scaled = center * lax.rsqrt(lax.optimization_barrier(jnp.mean(center * center, axis=-1, keepdims=True)) + epsilon)
    return scaled * gain_row + bias_row

def slot_positions(routes_dev, expert_count, capacity):
    onehot = (routes_dev[:, :, None] == jnp.arange(expert_count, dtype=jnp.int32)[None, None, :]).astype(jnp.int32)
    per_token = lax.optimization_barrier(jnp.sum(onehot, axis=1))
    earlier = jnp.cumsum(per_token, axis=0) - per_token
    slots = lax.optimization_barrier(jnp.sum(earlier[:, None, :] * onehot, axis=-1))
    return (routes_dev * capacity + slots).astype(jnp.int32)

def reference(tokens, routes, cotangent, ln_gain, ln_bias, w_qkv, w_out, w_router, w_in, w_back):
    groups = N_FSDP * N_EXPERT
    positions = jax.vmap(lambda block_routes: slot_positions(block_routes, EXPERTS, CAP))(routes.reshape(groups, TOK_DEV, TOP))
    scale_factor = HEAD_DIM ** (-0.5)

    def fill_slots(rows_block, pos_block):
        base = jnp.zeros((EXPERTS * CAP, D), jnp.float32)
        return base.at[pos_block.reshape(-1)].set(jnp.repeat(rows_block, TOP, axis=0))

    def pick_slots(table, pos_block):
        return table[pos_block]

    def forward(residual, gain_all, bias_all, qkv_all, out_all, router_all, in_all, back_all):
        for layer_idx in range(LAYERS):
            normed = low(layer_norm(residual, gain_all[layer_idx, 0], bias_all[layer_idx, 0]))
            mixed_qkv = low(low_back(jnp.einsum('td,dcj->tcj', normed, qkv_all[layer_idx], precision=highest)))
            heads_view = mixed_qkv.reshape(IMAGES, SEQ, 3, HEADS, HEAD_DIM)
            queries = heads_view[:, :, 0]
            keys_all = heads_view[:, :, 1]
            values_all = heads_view[:, :, 2]
            scores = low_back(jnp.einsum('ishd,ithd->ihst', queries, keys_all, precision=highest) * scale_factor)
            probs = low(jax.nn.softmax(scores, axis=-1))
            attended = jnp.einsum('ihst,ithd->ishd', probs, values_all, precision=highest).reshape(TOKENS, D)
            attended = low(low_back(attended))
            branch = low_back(jnp.dot(attended, out_all[layer_idx], precision=highest))
            middle = residual + branch
            routed = low(layer_norm(middle, gain_all[layer_idx, 1], bias_all[layer_idx, 1]))
            logits = low_back(jnp.dot(routed, router_all[layer_idx], precision=highest))
            gate_probs = jax.nn.softmax(logits, axis=-1)
            combine = jnp.take_along_axis(gate_probs, routes, axis=1).reshape(groups, TOK_DEV, TOP)
            buffers = jax.vmap(fill_slots)(routed.reshape(groups, TOK_DEV, D), positions)
            buffers = low_back(buffers)
            expert_in = buffers.reshape(groups, EXPERTS, CAP, D).transpose(1, 0, 2, 3).reshape(EXPERTS, groups * CAP, D)
            pre_act = low_back(jnp.einsum('erd,edf->erf', expert_in, in_all[layer_idx], precision=highest))
            hidden = low(jax.nn.gelu(pre_act, approximate=False))
            expert_out = low(low_back(jnp.einsum('erf,efd->erd', hidden, back_all[layer_idx], precision=highest)))
            table = expert_out.reshape(EXPERTS, groups, CAP, D).transpose(1, 0, 2, 3).reshape(groups, EXPERTS * CAP, D)
            picked = jax.vmap(pick_slots)(table, positions)
            mixture = lax.optimization_barrier(jnp.sum(combine[:, :, :, None] * picked, axis=2)).reshape(TOKENS, D)
            residual = middle + mixture
        return residual
    floats = (tokens, ln_gain, ln_bias, w_qkv, w_out, w_router, w_in, w_back)
    floats = tuple((item.astype(jnp.float32) for item in floats))
    result, pull = jax.vjp(forward, *floats)
    grads = pull(cotangent.astype(jnp.float32))
    return (result.astype(jnp.bfloat16), grads[0], grads[1], grads[2], grads[3], grads[4], grads[5], grads[6], grads[7])
```

```python
import jax
import jax.numpy as jnp
from jax import lax
from jax.sharding import PartitionSpec as P

HEAD_DIM = 64
SEQ = 197
ROW_TILE = 16

epsilon = 1e-06


def layer_norm(values, gain_row, bias_row):
    center = values - jnp.mean(values, axis=-1, keepdims=True)
    inverse = lax.rsqrt(jnp.mean(center * center, axis=-1, keepdims=True) + epsilon)
    scaled = center * inverse
    return (scaled * gain_row + bias_row, scaled, inverse)


def norm_back(grad_out, scaled, inverse, gain_row):
    grad_scaled = grad_out * gain_row
    grad_values = inverse * (
        grad_scaled
        - jnp.mean(grad_scaled, axis=-1, keepdims=True)
        - scaled * jnp.mean(grad_scaled * scaled, axis=-1, keepdims=True)
    )
    return (grad_values, jnp.sum(grad_out * scaled, axis=0), jnp.sum(grad_out, axis=0))


def slot_positions(routes_dev, expert_count, capacity):
    onehot = (
        routes_dev[:, :, None] == jnp.arange(expert_count, dtype=jnp.int32)[None, None, :]
    ).astype(jnp.int32)
    per_token = jnp.sum(onehot, axis=1)
    earlier = jnp.cumsum(per_token, axis=0) - per_token
    slots = jnp.sum(earlier[:, None, :] * onehot, axis=-1)
    return routes_dev * capacity + slots


def move_rows(buffer, experts):
    rows, cols = buffer.shape
    moved = lax.all_to_all(
        buffer.reshape(experts, rows // experts, cols),
        ("fsdp", "expert"),
        split_axis=0,
        concat_axis=0,
        tiled=True,
    )
    return moved.reshape(rows, cols)


def plain_dot(left, right):
    return jnp.dot(left, right, preferred_element_type=jnp.float32)


def contract_first(left, right):
    return lax.dot_general(
        left, right, (((0,), (0,)), ((), ())), preferred_element_type=jnp.float32
    )


def contract_last(left, right):
    return lax.dot_general(
        left, right, (((1,), (1,)), ((), ())), preferred_element_type=jnp.float32
    )


def gather_layer(w_qkv_layer, w_out_layer, fsdp_width, tensor_width):
    rows, _, cols = w_qkv_layer.shape
    packed = jnp.concatenate([w_qkv_layer.reshape(rows, 3 * cols), w_out_layer], axis=1)
    full = lax.all_gather(packed, ("fsdp", "tensor"), axis=0, tiled=True)
    full = full.reshape(fsdp_width, tensor_width, rows, 4, cols)
    qkv = full[:, :, :, :3].transpose(0, 2, 3, 1, 4)
    qkv = qkv.reshape(fsdp_width * rows, 3 * tensor_width * cols)
    out = full[:, :, :, 3].transpose(1, 2, 0, 3)
    return qkv, out.reshape(tensor_width * rows, fsdp_width * cols)


def scatter_layer(grad_qkv, grad_out, fsdp_width, tensor_width):
    feat = grad_qkv.shape[0]
    rows, cols = feat // fsdp_width, feat // tensor_width
    qkv = grad_qkv.astype(jnp.bfloat16).reshape(fsdp_width, rows, 3, tensor_width, cols)
    qkv = qkv.transpose(0, 3, 1, 2, 4).reshape(fsdp_width, tensor_width, rows, 3 * cols)
    out = grad_out.astype(jnp.bfloat16).reshape(tensor_width, cols, fsdp_width, rows)
    out = out.transpose(2, 0, 1, 3)
    packed = jnp.concatenate([qkv, out], axis=3).reshape(-1, 4 * cols)
    part = lax.psum_scatter(
        packed, ("fsdp", "tensor"), scatter_dimension=0, tiled=True
    ).astype(jnp.float32)
    part = lax.psum(part, "expert")
    return part[:, : 3 * cols].reshape(rows, 3, cols), part[:, 3 * cols :]


def on_device(tokens, routes, cotangent, ln_gain, ln_bias, w_qkv, w_out, w_router, w_in, w_back):
    tok_rows, feat = tokens.shape
    top_count = routes.shape[1]
    fsdp_width = lax.axis_size("fsdp")
    experts = lax.axis_size(("fsdp", "expert"))
    tensor_width = lax.axis_size("tensor")
    capacity = (3 * tok_rows * top_count // (2 * experts) + 7) // 8 * 8
    slot_rows = experts * capacity
    images = tok_rows // SEQ
    own_images = images // tensor_width
    padded = (SEQ + ROW_TILE - 1) // ROW_TILE * ROW_TILE
    own_rows = own_images * padded
    heads = feat // HEAD_DIM
    scale_factor = HEAD_DIM ** (-0.5)
    layer_count = w_qkv.shape[0]
    low = jnp.bfloat16
    share = lax.axis_index("tensor")

    def pad_images(array, fill):
        array = array.reshape(images, SEQ, array.shape[1])
        array = jnp.pad(
            array, ((0, 0), (0, padded - SEQ), (0, 0)), constant_values=fill
        )
        return array.reshape(images * padded, array.shape[2])

    def drop_padding(array):
        array = array.reshape(images, padded, array.shape[1])[:, :SEQ]
        return array.reshape(tok_rows, array.shape[2])

    def own_part(array):
        return lax.dynamic_slice_in_dim(array, share * own_rows, own_rows, 0)

    def all_tokens(array):
        return lax.all_gather(array, "tensor", axis=0, tiled=True)

    def sum_own(array):
        return lax.psum_scatter(array, "tensor", scatter_dimension=0, tiled=True)

    weights = [
        gather_layer(w_qkv[layer], w_out[layer], fsdp_width, tensor_width)
        for layer in range(layer_count)
    ]
    local_feat = w_router.shape[1]
    small = jnp.concatenate(
        [
            w_router.transpose(0, 2, 1).reshape(layer_count * experts, local_feat),
            ln_gain.reshape(2 * layer_count, local_feat),
            ln_bias.reshape(2 * layer_count, local_feat),
        ],
        axis=0,
    )
    small = lax.all_gather(small, "fsdp", axis=1, tiled=True)
    router_all = small[: layer_count * experts].reshape(layer_count, experts, feat)
    norms = small[layer_count * experts :].astype(jnp.float32)
    norms = norms.reshape(2, layer_count, 2, feat)

    positions = slot_positions(pad_images(routes, -1), experts, capacity)
    slot_ids = jnp.arange(slot_rows, dtype=jnp.int32)[:, None]
    dispatch = (
        (positions[None, :, 0] == slot_ids) | (positions[None, :, 1] == slot_ids)
    ).astype(low)
    slot_expert = (
        (slot_ids // capacity) == jnp.arange(experts, dtype=jnp.int32)[None, :]
    ).astype(jnp.float32)
    key_bias = jnp.where(jnp.arange(padded) < SEQ, 0.0, -1e30).astype(jnp.float32)

    def split_heads(array):
        array = array.reshape(own_images, padded, heads, HEAD_DIM)
        return array.transpose(0, 2, 1, 3)

    def join_heads(array):
        return array.transpose(0, 2, 1, 3).reshape(own_rows, feat)

    residual = own_part(pad_images(tokens, 0)).astype(jnp.float32)
    kept_layer = []
    for layer in range(layer_count):
        weight_qkv, weight_out = weights[layer]
        router_rows = router_all[layer]
        gain_pair = norms[0, layer]
        bias_pair = norms[1, layer]
        normed, scaled_first, inverse_first = layer_norm(residual, gain_pair[0], bias_pair[0])
        normed = normed.astype(low)
        mixed = plain_dot(normed, weight_qkv).astype(low)
        queries = split_heads(mixed[:, :feat])
        keys_all = split_heads(mixed[:, feat : 2 * feat])
        values_all = split_heads(mixed[:, 2 * feat :])
        scores = (
            jnp.einsum("ihsd,ihtd->ihst", queries, keys_all, preferred_element_type=jnp.float32)
            * scale_factor
            + key_bias
        )
        grown = jnp.exp(scores - jnp.max(scores, axis=-1, keepdims=True))
        probs_full = grown / jnp.sum(grown, axis=-1, keepdims=True)
        probs_low = probs_full.astype(low)
        attended = join_heads(
            jnp.einsum(
                "ihst,ihtd->ihsd", probs_low, values_all, preferred_element_type=jnp.float32
            ).astype(low)
        )
        middle = residual + plain_dot(attended, weight_out)
        routed, scaled_second, inverse_second = layer_norm(middle, gain_pair[1], bias_pair[1])
        routed = routed.astype(low)
        gate_probs = jax.nn.softmax(contract_last(routed, router_rows), axis=-1)
        buffer = plain_dot(dispatch, all_tokens(routed)).astype(low)
        arrived = move_rows(buffer, experts)
        slot_gates = jax.nn.softmax(contract_last(buffer, router_rows), axis=-1)
        slot_combine = jnp.sum(slot_gates * slot_expert, axis=-1, keepdims=True)
        pre_act = plain_dot(arrived, w_in[layer, 0])
        hidden = jax.nn.gelu(pre_act, approximate=False).astype(low)
        partial_out = plain_dot(hidden, w_back[layer, 0]).astype(low)
        returned = move_rows(partial_out, experts)
        weighted = (slot_combine * returned.astype(jnp.float32)).astype(low)
        mixture = sum_own(contract_first(dispatch, weighted).astype(low))
        kept_layer.append(
            (
                normed,
                scaled_first,
                inverse_first,
                queries,
                keys_all,
                values_all,
                probs_full,
                attended,
                routed,
                scaled_second,
                inverse_second,
                gate_probs,
                slot_combine,
                arrived,
                pre_act,
                hidden,
                returned,
            )
        )
        residual = middle + mixture.astype(jnp.float32)
    output = drop_padding(all_tokens(residual.astype(low)))

    grad_all = pad_images(cotangent, 0)
    grad_res = own_part(grad_all).astype(jnp.float32)
    gain_grads = [None] * layer_count
    bias_grads = [None] * layer_count
    router_grads = [None] * layer_count
    qkv_grads = [None] * layer_count
    out_grads = [None] * layer_count
    in_grads = [None] * layer_count
    back_grads = [None] * layer_count
    for layer in reversed(range(layer_count)):
        (
            normed,
            scaled_first,
            inverse_first,
            queries,
            keys_all,
            values_all,
            probs_full,
            attended,
            routed,
            scaled_second,
            inverse_second,
            gate_probs,
            slot_combine,
            arrived,
            pre_act,
            hidden,
            returned,
        ) = kept_layer[layer]
        weight_qkv, weight_out = weights[layer]
        router_rows = router_all[layer]
        gain_pair = norms[0, layer]
        if grad_all is None:
            grad_all = all_tokens(grad_res.astype(low))
        grad_buffer = (slot_combine * plain_dot(dispatch, grad_all)).astype(low)
        grad_slots = move_rows(grad_buffer, experts)
        slot_dots = jnp.sum(
            returned.astype(jnp.float32) * grad_buffer.astype(jnp.float32), axis=-1, keepdims=True
        )
        spread_dots = slot_dots * slot_expert
        dots_high = spread_dots.astype(low)
        dots_low = (spread_dots - dots_high.astype(jnp.float32)).astype(low)
        gate_dots = contract_first(dispatch, jnp.concatenate([dots_high, dots_low], axis=1))
        gate_dots = sum_own(gate_dots[:, :experts] + gate_dots[:, experts:])
        weight_back = w_back[layer, 0]
        weight_in = w_in[layer, 0]
        grad_hidden = contract_last(grad_slots, weight_back)
        _, gelu_pull = jax.vjp(lambda value: jax.nn.gelu(value, approximate=False), pre_act)
        grad_pre = gelu_pull(grad_hidden)[0].astype(low)
        partial_in = contract_last(grad_pre, weight_in).astype(low)
        grad_returned = move_rows(partial_in, experts)
        back_grads[layer] = contract_first(hidden, grad_slots)
        in_grads[layer] = contract_first(arrived, grad_pre)
        grad_routed = sum_own(contract_first(dispatch, grad_returned).astype(low))
        grad_routed = grad_routed.astype(jnp.float32)
        grad_logits = (
            gate_dots - gate_probs * jnp.sum(gate_dots, axis=-1, keepdims=True)
        ).astype(low)
        router_grads[layer] = contract_first(grad_logits, routed)
        grad_routed = grad_routed + plain_dot(grad_logits, router_rows)
        grad_norm_two, gain_two, bias_two = norm_back(
            grad_routed, scaled_second, inverse_second, gain_pair[1]
        )
        grad_middle = grad_res + grad_norm_two
        grad_branch = grad_middle.astype(low)
        out_grads[layer] = contract_first(attended, grad_branch)
        grad_attended = split_heads(contract_last(grad_branch, weight_out).astype(low))
        grad_values = jnp.einsum(
            "ihst,ihsd->ihtd",
            probs_full.astype(low),
            grad_attended,
            preferred_element_type=jnp.float32,
        )
        grad_probs = jnp.einsum(
            "ihsd,ihtd->ihst", grad_attended, values_all, preferred_element_type=jnp.float32
        )
        grad_scores = (
            probs_full * (grad_probs - jnp.sum(probs_full * grad_probs, axis=-1, keepdims=True))
        ).astype(low)
        grad_queries = (
            jnp.einsum(
                "ihst,ihtd->ihsd", grad_scores, keys_all, preferred_element_type=jnp.float32
            )
            * scale_factor
        )
        grad_keys = (
            jnp.einsum("ihst,ihsd->ihtd", grad_scores, queries, preferred_element_type=jnp.float32)
            * scale_factor
        )
        grad_mixed = jnp.concatenate(
            [
                join_heads(grad_queries.astype(low)),
                join_heads(grad_keys.astype(low)),
                join_heads(grad_values.astype(low)),
            ],
            axis=1,
        )
        grad_normed = contract_last(grad_mixed, weight_qkv)
        grad_norm_one, gain_one, bias_one = norm_back(
            grad_normed, scaled_first, inverse_first, gain_pair[0]
        )
        grad_res = grad_middle + grad_norm_one
        grad_all = None
        qkv_grads[layer], out_grads[layer] = scatter_layer(
            contract_first(normed, grad_mixed), out_grads[layer], fsdp_width, tensor_width
        )
        gain_grads[layer] = jnp.stack([gain_one, gain_two], axis=0)
        bias_grads[layer] = jnp.stack([bias_one, bias_two], axis=0)
    grad_tokens = drop_padding(all_tokens(grad_res.astype(low)).astype(jnp.float32))
    small_grads = jnp.concatenate(router_grads + gain_grads + bias_grads, axis=0)
    small_grads = lax.psum(small_grads, ("fsdp", "expert", "tensor"))
    small_grads = lax.dynamic_slice_in_dim(
        small_grads, lax.axis_index("fsdp") * local_feat, local_feat, 1
    )
    split = layer_count * experts
    grad_router = small_grads[:split].reshape(layer_count, experts, local_feat)
    grad_gain = small_grads[split : split + 2 * layer_count]
    grad_bias = small_grads[split + 2 * layer_count :]
    return (
        output,
        grad_tokens,
        grad_gain.reshape(layer_count, 2, local_feat),
        grad_bias.reshape(layer_count, 2, local_feat),
        jnp.stack(qkv_grads),
        jnp.stack(out_grads),
        grad_router.transpose(0, 2, 1),
        jnp.stack(in_grads)[:, None],
        jnp.stack(back_grads)[:, None],
    )


def solution(mesh):
    in_specs = (
        P(("fsdp", "expert"), None),
        P(("fsdp", "expert"), None),
        P(("fsdp", "expert"), None),
        P(None, None, "fsdp"),
        P(None, None, "fsdp"),
        P(None, "fsdp", None, "tensor"),
        P(None, "tensor", "fsdp"),
        P(None, "fsdp", None),
        P(None, ("fsdp", "expert"), None, "tensor"),
        P(None, ("fsdp", "expert"), "tensor", None),
    )
    out_specs = (
        P(("fsdp", "expert"), None),
        P(("fsdp", "expert"), None),
        P(None, None, "fsdp"),
        P(None, None, "fsdp"),
        P(None, "fsdp", None, "tensor"),
        P(None, "tensor", "fsdp"),
        P(None, "fsdp", None),
        P(None, ("fsdp", "expert"), None, "tensor"),
        P(None, ("fsdp", "expert"), "tensor", None),
    )
    return jax.shard_map(
        on_device, mesh=mesh, in_specs=in_specs, out_specs=out_specs, check_vma=False
    )
```

```python
import jax
import jax.numpy as jnp
from jax import lax
from jax.sharding import PartitionSpec as P

HEAD_DIM = 64
SEQ = 197
ROW_TILE = 16

epsilon = 1e-06


def layer_norm(values, gain_row, bias_row):
    center = values - jnp.mean(values, axis=-1, keepdims=True)
    inverse = lax.rsqrt(jnp.mean(center * center, axis=-1, keepdims=True) + epsilon)
    scaled = center * inverse
    return (scaled * gain_row + bias_row, scaled, inverse)


def norm_back(grad_out, scaled, inverse, gain_row):
    grad_scaled = grad_out * gain_row
    grad_values = inverse * (
        grad_scaled
        - jnp.mean(grad_scaled, axis=-1, keepdims=True)
        - scaled * jnp.mean(grad_scaled * scaled, axis=-1, keepdims=True)
    )
    return (grad_values, jnp.sum(grad_out * scaled, axis=0), jnp.sum(grad_out, axis=0))


def slot_positions(routes_dev, expert_count, capacity):
    onehot = (
        routes_dev[:, :, None] == jnp.arange(expert_count, dtype=jnp.int32)[None, None, :]
    ).astype(jnp.int32)
    per_token = jnp.sum(onehot, axis=1)
    earlier = jnp.cumsum(per_token, axis=0) - per_token
    slots = jnp.sum(earlier[:, None, :] * onehot, axis=-1)
    return routes_dev * capacity + slots


def move_rows(buffer, experts):
    rows, cols = buffer.shape
    moved = lax.all_to_all(
        buffer.reshape(experts, rows // experts, cols),
        ("fsdp", "expert"),
        split_axis=0,
        concat_axis=0,
        tiled=True,
    )
    return moved.reshape(rows, cols)


def plain_dot(left, right):
    return jnp.dot(left, right, preferred_element_type=jnp.float32)


def contract_first(left, right):
    return lax.dot_general(
        left, right, (((0,), (0,)), ((), ())), preferred_element_type=jnp.float32
    )


def contract_last(left, right):
    return lax.dot_general(
        left, right, (((1,), (1,)), ((), ())), preferred_element_type=jnp.float32
    )


def swap_cores(array):
    width = lax.axis_size("expert")
    pairs = [(core, width - 1 - core) for core in range(width)]
    return lax.ppermute(array, "expert", pairs)


def gather_layer(w_qkv_layer, w_out_layer):
    rows, _, cols = w_qkv_layer.shape
    packed = jnp.concatenate(
        [w_qkv_layer.reshape(rows, 3 * cols), w_out_layer.transpose(1, 0)], axis=1
    )
    tensor_width = lax.axis_size("tensor")
    full = lax.all_gather(packed, ("tensor", "fsdp"), axis=0, tiled=True)
    return full.reshape(tensor_width, -1, 4 * cols)


def scatter_layer(grad_packed, small_grads):
    tensor_width = lax.axis_size("tensor")
    fsdp_width = lax.axis_size("fsdp")
    cores = lax.axis_size("expert")
    _, feat, cols = grad_packed.shape
    rows = feat // fsdp_width
    half = rows // cores
    small_count = small_grads.shape[0]
    small = small_grads.reshape(small_count, fsdp_width, rows).transpose(1, 0, 2)
    small = small.reshape(fsdp_width, small_count * rows)
    small_rows = (small_count * rows + cols - 1) // cols
    small_rows = (small_rows + ROW_TILE - 1) // ROW_TILE * ROW_TILE
    small = jnp.pad(small, ((0, 0), (0, small_rows * cols - small_count * rows)))
    small = small.astype(jnp.bfloat16).reshape(1, fsdp_width, small_rows, cols)
    small = jnp.broadcast_to(small, (tensor_width, fsdp_width, small_rows, cols))
    split = grad_packed.astype(jnp.bfloat16).reshape(
        tensor_width, fsdp_width, cores, half, cols
    )
    core = lax.axis_index("expert")
    mine = lax.dynamic_index_in_dim(split, core, 2, keepdims=False)
    theirs = lax.dynamic_index_in_dim(split, 1 - core, 2, keepdims=False)
    chunk = half + small_rows
    mine = jnp.concatenate([mine, small], axis=2).reshape(-1, cols)
    theirs = jnp.concatenate([theirs, small], axis=2).reshape(-1, cols)
    both = mine.astype(jnp.float32) + swap_cores(theirs).astype(jnp.float32)
    part = lax.psum_scatter(
        both.astype(jnp.bfloat16), ("tensor", "fsdp"), scatter_dimension=0, tiled=True
    )
    small_sum = part[half:chunk].reshape(-1)[: small_count * rows]
    own_half = part[:half]
    other_half = swap_cores(own_half)
    upper = core == 1
    whole = jnp.concatenate(
        [jnp.where(upper, other_half, own_half), jnp.where(upper, own_half, other_half)], axis=0
    ).astype(jnp.float32)
    qkv_cols = cols // 4 * 3
    return (
        whole[:, :qkv_cols].reshape(rows, 3, qkv_cols // 3),
        whole[:, qkv_cols:].transpose(1, 0),
        small_sum.astype(jnp.float32).reshape(small_count, rows),
    )


def on_device(tokens, routes, cotangent, ln_gain, ln_bias, w_qkv, w_out, w_router, w_in, w_back):
    tok_rows, feat = tokens.shape
    top_count = routes.shape[1]
    experts = lax.axis_size(("fsdp", "expert"))
    tensor_width = lax.axis_size("tensor")
    capacity = (3 * tok_rows * top_count // (2 * experts) + 7) // 8 * 8
    slot_rows = experts * capacity
    images = tok_rows // SEQ
    own_images = images // tensor_width
    padded = (SEQ + ROW_TILE - 1) // ROW_TILE * ROW_TILE
    own_rows = own_images * padded
    share_cols = feat // tensor_width
    heads = share_cols // HEAD_DIM
    scale_factor = HEAD_DIM ** (-0.5)
    layer_count = w_qkv.shape[0]
    low = jnp.bfloat16
    share = lax.axis_index("tensor")

    def pad_images(array, fill):
        array = array.reshape(images, SEQ, array.shape[1])
        array = jnp.pad(
            array, ((0, 0), (0, padded - SEQ), (0, 0)), constant_values=fill
        )
        return array.reshape(images * padded, array.shape[2])

    def drop_padding(array):
        array = array.reshape(images, padded, array.shape[1])[:, :SEQ]
        return array.reshape(tok_rows, array.shape[2])

    def own_part(array):
        return lax.dynamic_slice_in_dim(array, share * own_rows, own_rows, 0)

    def all_tokens(array):
        return lax.all_gather(array, "tensor", axis=0, tiled=True)

    def sum_own(array):
        return lax.psum_scatter(array, "tensor", scatter_dimension=0, tiled=True)

    weights = [
        gather_layer(w_qkv[layer], w_out[layer]) for layer in range(layer_count)
    ]
    local_feat = w_router.shape[1]
    small = jnp.concatenate(
        [
            w_router.transpose(0, 2, 1).reshape(layer_count * experts, local_feat),
            ln_gain.reshape(2 * layer_count, local_feat),
            ln_bias.reshape(2 * layer_count, local_feat),
        ],
        axis=0,
    )
    small = lax.all_gather(small, "fsdp", axis=1, tiled=True)
    router_all = small[: layer_count * experts].reshape(layer_count, experts, feat)
    norms = small[layer_count * experts :].astype(jnp.float32)
    norms = norms.reshape(2, layer_count, 2, feat)

    positions = slot_positions(pad_images(routes, -1), experts, capacity)
    slot_ids = jnp.arange(slot_rows, dtype=jnp.int32)[:, None]
    dispatch = (
        (positions[None, :, 0] == slot_ids) | (positions[None, :, 1] == slot_ids)
    ).astype(low)
    slot_expert = (
        (slot_ids // capacity) == jnp.arange(experts, dtype=jnp.int32)[None, :]
    ).astype(jnp.float32)
    key_bias = jnp.where(jnp.arange(padded) < SEQ, 0.0, -1e30).astype(jnp.float32)

    def split_heads(array):
        array = array.reshape(tensor_width, own_images, padded, -1, heads, HEAD_DIM)
        return array.transpose(3, 0, 1, 4, 2, 5)

    def join_heads(array):
        array = array.transpose(0, 1, 3, 2, 4)
        return array.reshape(tensor_width, own_rows, share_cols)

    residual = own_part(pad_images(tokens, 0)).astype(jnp.float32)
    kept_layer = []
    for layer in range(layer_count):
        weight = weights[layer]
        weight_qkv = weight[:, :, : 3 * share_cols]
        weight_out = weight[:, :, 3 * share_cols :]
        router_rows = router_all[layer]
        gain_pair = norms[0, layer]
        bias_pair = norms[1, layer]
        normed, scaled_first, inverse_first = layer_norm(residual, gain_pair[0], bias_pair[0])
        normed = normed.astype(low)
        mixed = jnp.stack([plain_dot(normed, part) for part in weight_qkv]).astype(low)
        queries, keys_all, values_all = split_heads(mixed)
        scores = (
            jnp.einsum("gihsd,gihtd->gihst", queries, keys_all, preferred_element_type=jnp.float32)
            * scale_factor
            + key_bias
        )
        grown = jnp.exp(scores - jnp.max(scores, axis=-1, keepdims=True))
        probs_full = grown / jnp.sum(grown, axis=-1, keepdims=True)
        probs_low = probs_full.astype(low)
        attended = join_heads(
            jnp.einsum(
                "gihst,gihtd->gihsd", probs_low, values_all, preferred_element_type=jnp.float32
            ).astype(low)
        )
        middle = residual
        for part in range(tensor_width):
            middle = middle + contract_last(attended[part], weight_out[part])
        routed, scaled_second, inverse_second = layer_norm(middle, gain_pair[1], bias_pair[1])
        routed = routed.astype(low)
        gate_probs = jax.nn.softmax(contract_last(routed, router_rows), axis=-1)
        buffer = plain_dot(dispatch, all_tokens(routed)).astype(low)
        arrived = move_rows(buffer, experts)
        slot_gates = jax.nn.softmax(contract_last(buffer, router_rows), axis=-1)
        slot_combine = jnp.sum(slot_gates * slot_expert, axis=-1, keepdims=True)
        pre_act = plain_dot(arrived, w_in[layer, 0])
        hidden = jax.nn.gelu(pre_act, approximate=False).astype(low)
        partial_out = plain_dot(hidden, w_back[layer, 0]).astype(low)
        returned = move_rows(partial_out, experts)
        weighted = (slot_combine * returned.astype(jnp.float32)).astype(low)
        mixture = sum_own(contract_first(dispatch, weighted).astype(low))
        kept_layer.append(
            (
                normed,
                scaled_first,
                inverse_first,
                queries,
                keys_all,
                values_all,
                probs_full,
                attended,
                routed,
                scaled_second,
                inverse_second,
                gate_probs,
                slot_combine,
                arrived,
                pre_act,
                hidden,
                returned,
            )
        )
        residual = middle + mixture.astype(jnp.float32)
    output = drop_padding(all_tokens(residual.astype(low)))

    grad_all = pad_images(cotangent, 0)
    grad_res = own_part(grad_all).astype(jnp.float32)
    small_grads = [None] * layer_count
    qkv_grads = [None] * layer_count
    out_grads = [None] * layer_count
    in_grads = [None] * layer_count
    back_grads = [None] * layer_count
    for layer in reversed(range(layer_count)):
        (
            normed,
            scaled_first,
            inverse_first,
            queries,
            keys_all,
            values_all,
            probs_full,
            attended,
            routed,
            scaled_second,
            inverse_second,
            gate_probs,
            slot_combine,
            arrived,
            pre_act,
            hidden,
            returned,
        ) = kept_layer[layer]
        weight = weights[layer]
        weight_qkv = weight[:, :, : 3 * share_cols]
        weight_out = weight[:, :, 3 * share_cols :]
        router_rows = router_all[layer]
        gain_pair = norms[0, layer]
        if grad_all is None:
            grad_all = all_tokens(grad_res.astype(low))
        grad_buffer = (slot_combine * plain_dot(dispatch, grad_all)).astype(low)
        grad_slots = move_rows(grad_buffer, experts)
        slot_dots = jnp.sum(
            returned.astype(jnp.float32) * grad_buffer.astype(jnp.float32), axis=-1, keepdims=True
        )
        spread_dots = slot_dots * slot_expert
        dots_high = spread_dots.astype(low)
        dots_low = (spread_dots - dots_high.astype(jnp.float32)).astype(low)
        gate_dots = contract_first(dispatch, jnp.concatenate([dots_high, dots_low], axis=1))
        gate_dots = sum_own(gate_dots[:, :experts] + gate_dots[:, experts:])
        weight_back = w_back[layer, 0]
        weight_in = w_in[layer, 0]
        grad_hidden = contract_last(grad_slots, weight_back)
        _, gelu_pull = jax.vjp(lambda value: jax.nn.gelu(value, approximate=False), pre_act)
        grad_pre = gelu_pull(grad_hidden)[0].astype(low)
        partial_in = contract_last(grad_pre, weight_in).astype(low)
        grad_returned = move_rows(partial_in, experts)
        back_grads[layer] = contract_first(hidden, grad_slots)
        in_grads[layer] = contract_first(arrived, grad_pre)
        grad_routed = sum_own(contract_first(dispatch, grad_returned).astype(low))
        grad_routed = grad_routed.astype(jnp.float32)
        grad_logits = (
            gate_dots - gate_probs * jnp.sum(gate_dots, axis=-1, keepdims=True)
        ).astype(low)
        router_grad = contract_first(grad_logits, routed)
        grad_routed = grad_routed + plain_dot(grad_logits, router_rows)
        grad_norm_two, gain_two, bias_two = norm_back(
            grad_routed, scaled_second, inverse_second, gain_pair[1]
        )
        grad_middle = grad_res + grad_norm_two
        grad_branch = grad_middle.astype(low)
        grad_out = jnp.stack([contract_first(grad_branch, part) for part in attended])
        grad_attended = jnp.stack([plain_dot(grad_branch, part) for part in weight_out])
        grad_attended = split_heads(grad_attended.astype(low))[0]
        grad_values = jnp.einsum(
            "gihst,gihsd->gihtd",
            probs_full.astype(low),
            grad_attended,
            preferred_element_type=jnp.float32,
        )
        grad_probs = jnp.einsum(
            "gihsd,gihtd->gihst", grad_attended, values_all, preferred_element_type=jnp.float32
        )
        grad_scores = (
            probs_full * (grad_probs - jnp.sum(probs_full * grad_probs, axis=-1, keepdims=True))
        ).astype(low)
        grad_queries = (
            jnp.einsum(
                "gihst,gihtd->gihsd", grad_scores, keys_all, preferred_element_type=jnp.float32
            )
            * scale_factor
        )
        grad_keys = (
            jnp.einsum("gihst,gihsd->gihtd", grad_scores, queries, preferred_element_type=jnp.float32)
            * scale_factor
        )
        grad_mixed = jnp.concatenate(
            [
                join_heads(grad_queries.astype(low)),
                join_heads(grad_keys.astype(low)),
                join_heads(grad_values.astype(low)),
            ],
            axis=2,
        )
        grad_normed = sum(
            contract_last(grad_mixed[part], weight_qkv[part]) for part in range(tensor_width)
        )
        grad_norm_one, gain_one, bias_one = norm_back(
            grad_normed, scaled_first, inverse_first, gain_pair[0]
        )
        grad_res = grad_middle + grad_norm_one
        grad_all = None
        grad_qkv = jnp.stack([contract_first(normed, part) for part in grad_mixed])
        qkv_grads[layer], out_grads[layer], small_grads[layer] = scatter_layer(
            jnp.concatenate([grad_qkv.astype(low), grad_out.astype(low)], axis=2),
            jnp.concatenate(
                [router_grad, jnp.stack([gain_one, gain_two, bias_one, bias_two])], axis=0
            ),
        )
    grad_tokens = drop_padding(all_tokens(grad_res.astype(low)).astype(jnp.float32))
    small_all = jnp.stack(small_grads)
    grad_router = small_all[:, :experts]
    grad_gain = small_all[:, experts : experts + 2]
    grad_bias = small_all[:, experts + 2 :]
    return (
        output,
        grad_tokens,
        grad_gain,
        grad_bias,
        jnp.stack(qkv_grads),
        jnp.stack(out_grads),
        grad_router.transpose(0, 2, 1),
        jnp.stack(in_grads)[:, None],
        jnp.stack(back_grads)[:, None],
    )


def solution(mesh):
    in_specs = (
        P(("fsdp", "expert"), None),
        P(("fsdp", "expert"), None),
        P(("fsdp", "expert"), None),
        P(None, None, "fsdp"),
        P(None, None, "fsdp"),
        P(None, "fsdp", None, "tensor"),
        P(None, "tensor", "fsdp"),
        P(None, "fsdp", None),
        P(None, ("fsdp", "expert"), None, "tensor"),
        P(None, ("fsdp", "expert"), "tensor", None),
    )
    out_specs = (
        P(("fsdp", "expert"), None),
        P(("fsdp", "expert"), None),
        P(None, None, "fsdp"),
        P(None, None, "fsdp"),
        P(None, "fsdp", None, "tensor"),
        P(None, "tensor", "fsdp"),
        P(None, "fsdp", None),
        P(None, ("fsdp", "expert"), None, "tensor"),
        P(None, ("fsdp", "expert"), "tensor", None),
    )
    return jax.shard_map(
        on_device, mesh=mesh, in_specs=in_specs, out_specs=out_specs, check_vma=False
    )
```

```python
import jax
import jax.numpy as jnp
from jax import lax
from jax.sharding import PartitionSpec as P

HEAD_DIM = 64
SEQ = 197
ROW_TILE = 16

epsilon = 1e-06


def layer_norm(values, gain_row, bias_row):
    center = values - jnp.mean(values, axis=-1, keepdims=True)
    inverse = lax.rsqrt(jnp.mean(center * center, axis=-1, keepdims=True) + epsilon)
    scaled = center * inverse
    return (scaled * gain_row + bias_row, scaled, inverse)


def norm_back(grad_out, scaled, inverse, gain_row):
    grad_scaled = grad_out * gain_row
    grad_values = inverse * (
        grad_scaled
        - jnp.mean(grad_scaled, axis=-1, keepdims=True)
        - scaled * jnp.mean(grad_scaled * scaled, axis=-1, keepdims=True)
    )
    return (grad_values, jnp.sum(grad_out * scaled, axis=0), jnp.sum(grad_out, axis=0))


def slot_positions(routes_dev, expert_count, capacity):
    onehot = (
        routes_dev[:, :, None] == jnp.arange(expert_count, dtype=jnp.int32)[None, None, :]
    ).astype(jnp.int32)
    per_token = jnp.sum(onehot, axis=1)
    earlier = jnp.cumsum(per_token, axis=0) - per_token
    slots = jnp.sum(earlier[:, None, :] * onehot, axis=-1)
    return routes_dev * capacity + slots


def move_rows(buffer, experts):
    rows, cols = buffer.shape
    moved = lax.all_to_all(
        buffer.reshape(experts, rows // experts, cols),
        ("fsdp", "expert"),
        split_axis=0,
        concat_axis=0,
        tiled=True,
    )
    return moved.reshape(rows, cols)


def plain_dot(left, right):
    return jnp.dot(left, right, preferred_element_type=jnp.float32)


def contract_first(left, right):
    return lax.dot_general(
        left, right, (((0,), (0,)), ((), ())), preferred_element_type=jnp.float32
    )


def contract_last(left, right):
    return lax.dot_general(
        left, right, (((1,), (1,)), ((), ())), preferred_element_type=jnp.float32
    )


def swap_cores(array):
    width = lax.axis_size("expert")
    pairs = [(core, width - 1 - core) for core in range(width)]
    return lax.ppermute(array, "expert", pairs)


def gather_layer(w_qkv_layer, w_out_layer):
    rows, _, cols = w_qkv_layer.shape
    packed = jnp.concatenate(
        [w_qkv_layer.reshape(rows, 3 * cols), w_out_layer.transpose(1, 0)], axis=1
    )
    tensor_width = lax.axis_size("tensor")
    full = lax.all_gather(packed, ("tensor", "fsdp"), axis=0, tiled=True)
    return full.reshape(tensor_width, -1, 4 * cols)


def scatter_layer(grad_packed, small_grads):
    tensor_width = lax.axis_size("tensor")
    fsdp_width = lax.axis_size("fsdp")
    cores = lax.axis_size("expert")
    _, feat, cols = grad_packed.shape
    rows = feat // fsdp_width
    half = rows // cores
    small_count = small_grads.shape[0]
    small = small_grads.reshape(small_count, fsdp_width, rows).transpose(1, 0, 2)
    small = small.reshape(fsdp_width, small_count * rows)
    small_rows = (small_count * rows + cols - 1) // cols
    small_rows = (small_rows + ROW_TILE - 1) // ROW_TILE * ROW_TILE
    small = jnp.pad(small, ((0, 0), (0, small_rows * cols - small_count * rows)))
    small = small.astype(jnp.bfloat16).reshape(1, fsdp_width, small_rows, cols)
    small = jnp.broadcast_to(small, (tensor_width, fsdp_width, small_rows, cols))
    split = grad_packed.astype(jnp.bfloat16).reshape(
        tensor_width, fsdp_width, cores, half, cols
    )
    core = lax.axis_index("expert")
    chunk = half + small_rows
    if cores == 2:
        mine = lax.dynamic_index_in_dim(split, core, 2, keepdims=False)
        theirs = lax.dynamic_index_in_dim(split, 1 - core, 2, keepdims=False)
        mine = jnp.concatenate([mine, small], axis=2).reshape(-1, cols)
        theirs = jnp.concatenate([theirs, small], axis=2).reshape(-1, cols)
        both = mine.astype(jnp.float32) + swap_cores(theirs).astype(jnp.float32)
        both = both.astype(jnp.bfloat16)
    else:
        small = jnp.broadcast_to(
            small[None], (cores, tensor_width, fsdp_width, small_rows, cols)
        )
        every = jnp.concatenate([split.transpose(2, 0, 1, 3, 4), small], axis=3)
        both = lax.psum_scatter(
            every.reshape(-1, cols), "expert", scatter_dimension=0, tiled=True
        )
    both = both.reshape(tensor_width, fsdp_width, chunk, cols)
    both = lax.all_to_all(both, "fsdp", split_axis=1, concat_axis=1, tiled=True)
    both = jnp.sum(both.astype(jnp.float32), axis=1).astype(jnp.bfloat16)
    part = lax.psum_scatter(
        both.reshape(-1, cols), "tensor", scatter_dimension=0, tiled=True
    )
    small_sum = part[half:chunk].reshape(-1)[: small_count * rows]
    own_half = part[:half]
    if cores == 2:
        other_half = swap_cores(own_half)
        upper = core == 1
        whole = jnp.concatenate(
            [jnp.where(upper, other_half, own_half), jnp.where(upper, own_half, other_half)],
            axis=0,
        )
    else:
        whole = lax.all_gather(own_half, "expert", axis=0, tiled=True)
    whole = whole.astype(jnp.float32)
    qkv_cols = cols // 4 * 3
    return (
        whole[:, :qkv_cols].reshape(rows, 3, qkv_cols // 3),
        whole[:, qkv_cols:].transpose(1, 0),
        small_sum.astype(jnp.float32).reshape(small_count, rows),
    )


def on_device(tokens, routes, cotangent, ln_gain, ln_bias, w_qkv, w_out, w_router, w_in, w_back):
    tok_rows, feat = tokens.shape
    top_count = routes.shape[1]
    experts = lax.axis_size(("fsdp", "expert"))
    tensor_width = lax.axis_size("tensor")
    capacity = (3 * tok_rows * top_count // (2 * experts) + 7) // 8 * 8
    slot_rows = experts * capacity
    images = tok_rows // SEQ
    own_images = images // tensor_width
    padded = (SEQ + ROW_TILE - 1) // ROW_TILE * ROW_TILE
    own_rows = own_images * padded
    share_cols = feat // tensor_width
    heads = share_cols // HEAD_DIM
    scale_factor = HEAD_DIM ** (-0.5)
    layer_count = w_qkv.shape[0]
    low = jnp.bfloat16
    share = lax.axis_index("tensor")

    def pad_images(array, fill):
        array = array.reshape(images, SEQ, array.shape[1])
        array = jnp.pad(
            array, ((0, 0), (0, padded - SEQ), (0, 0)), constant_values=fill
        )
        return array.reshape(images * padded, array.shape[2])

    def drop_padding(array):
        array = array.reshape(images, padded, array.shape[1])[:, :SEQ]
        return array.reshape(tok_rows, array.shape[2])

    def own_part(array):
        return lax.dynamic_slice_in_dim(array, share * own_rows, own_rows, 0)

    def all_tokens(array):
        return lax.all_gather(array, "tensor", axis=0, tiled=True)

    def sum_own(array):
        return lax.psum_scatter(array, "tensor", scatter_dimension=0, tiled=True)

    weights = [
        gather_layer(w_qkv[layer], w_out[layer]) for layer in range(layer_count)
    ]
    local_feat = w_router.shape[1]
    small = jnp.concatenate(
        [
            w_router.transpose(0, 2, 1).reshape(layer_count * experts, local_feat),
            ln_gain.reshape(2 * layer_count, local_feat),
            ln_bias.reshape(2 * layer_count, local_feat),
        ],
        axis=0,
    )
    small = lax.all_gather(small, "fsdp", axis=1, tiled=True)
    router_all = small[: layer_count * experts].reshape(layer_count, experts, feat)
    norms = small[layer_count * experts :].astype(jnp.float32)
    norms = norms.reshape(2, layer_count, 2, feat)

    positions = slot_positions(pad_images(routes, -1), experts, capacity)
    slot_ids = jnp.arange(slot_rows, dtype=jnp.int32)[:, None]
    dispatch = (
        (positions[None, :, 0] == slot_ids) | (positions[None, :, 1] == slot_ids)
    ).astype(low)
    slot_expert = (
        (slot_ids // capacity) == jnp.arange(experts, dtype=jnp.int32)[None, :]
    ).astype(jnp.float32)
    key_bias = jnp.where(jnp.arange(padded) < SEQ, 0.0, -1e30).astype(jnp.float32)

    def split_heads(array):
        array = array.reshape(tensor_width, own_images, padded, -1, heads, HEAD_DIM)
        return array.transpose(3, 0, 1, 4, 2, 5)

    def join_heads(array):
        array = array.transpose(0, 1, 3, 2, 4)
        return array.reshape(tensor_width, own_rows, share_cols)

    residual = own_part(pad_images(tokens, 0)).astype(jnp.float32)
    kept_layer = []
    for layer in range(layer_count):
        weight = weights[layer]
        weight_qkv = weight[:, :, : 3 * share_cols]
        weight_out = weight[:, :, 3 * share_cols :]
        router_rows = router_all[layer]
        gain_pair = norms[0, layer]
        bias_pair = norms[1, layer]
        normed, scaled_first, inverse_first = layer_norm(residual, gain_pair[0], bias_pair[0])
        normed = normed.astype(low)
        mixed = jnp.stack([plain_dot(normed, part) for part in weight_qkv]).astype(low)
        queries, keys_all, values_all = split_heads(mixed)
        scores = (
            jnp.einsum("gihsd,gihtd->gihst", queries, keys_all, preferred_element_type=jnp.float32)
            * scale_factor
            + key_bias
        )
        grown = jnp.exp(scores - jnp.max(scores, axis=-1, keepdims=True))
        probs_full = grown / jnp.sum(grown, axis=-1, keepdims=True)
        probs_low = probs_full.astype(low)
        attended = join_heads(
            jnp.einsum(
                "gihst,gihtd->gihsd", probs_low, values_all, preferred_element_type=jnp.float32
            ).astype(low)
        )
        middle = residual
        for part in range(tensor_width):
            middle = middle + contract_last(attended[part], weight_out[part])
        routed, scaled_second, inverse_second = layer_norm(middle, gain_pair[1], bias_pair[1])
        routed = routed.astype(low)
        gate_probs = jax.nn.softmax(contract_last(routed, router_rows), axis=-1)
        buffer = plain_dot(dispatch, all_tokens(routed)).astype(low)
        arrived = move_rows(buffer, experts)
        slot_gates = jax.nn.softmax(contract_last(buffer, router_rows), axis=-1)
        slot_combine = jnp.sum(slot_gates * slot_expert, axis=-1, keepdims=True)
        pre_act = plain_dot(arrived, w_in[layer, 0])
        hidden = jax.nn.gelu(pre_act, approximate=False).astype(low)
        partial_out = plain_dot(hidden, w_back[layer, 0]).astype(low)
        returned = move_rows(partial_out, experts)
        weighted = (slot_combine * returned.astype(jnp.float32)).astype(low)
        mixture = sum_own(contract_first(dispatch, weighted).astype(low))
        kept_layer.append(
            (
                normed,
                scaled_first,
                inverse_first,
                queries,
                keys_all,
                values_all,
                probs_full,
                attended,
                routed,
                scaled_second,
                inverse_second,
                gate_probs,
                slot_combine,
                arrived,
                pre_act,
                hidden,
                returned,
            )
        )
        residual = middle + mixture.astype(jnp.float32)
    output = drop_padding(all_tokens(residual.astype(low)))

    grad_all = pad_images(cotangent, 0)
    grad_res = own_part(grad_all).astype(jnp.float32)
    small_grads = [None] * layer_count
    qkv_grads = [None] * layer_count
    out_grads = [None] * layer_count
    in_grads = [None] * layer_count
    back_grads = [None] * layer_count
    for layer in reversed(range(layer_count)):
        (
            normed,
            scaled_first,
            inverse_first,
            queries,
            keys_all,
            values_all,
            probs_full,
            attended,
            routed,
            scaled_second,
            inverse_second,
            gate_probs,
            slot_combine,
            arrived,
            pre_act,
            hidden,
            returned,
        ) = kept_layer[layer]
        weight = weights[layer]
        weight_qkv = weight[:, :, : 3 * share_cols]
        weight_out = weight[:, :, 3 * share_cols :]
        router_rows = router_all[layer]
        gain_pair = norms[0, layer]
        if grad_all is None:
            grad_all = all_tokens(grad_res.astype(low))
        grad_buffer = (slot_combine * plain_dot(dispatch, grad_all)).astype(low)
        grad_slots = move_rows(grad_buffer, experts)
        slot_dots = jnp.sum(
            returned.astype(jnp.float32) * grad_buffer.astype(jnp.float32), axis=-1, keepdims=True
        )
        spread_dots = slot_dots * slot_expert
        dots_high = spread_dots.astype(low)
        dots_low = (spread_dots - dots_high.astype(jnp.float32)).astype(low)
        gate_dots = contract_first(dispatch, jnp.concatenate([dots_high, dots_low], axis=1))
        gate_dots = sum_own(gate_dots[:, :experts] + gate_dots[:, experts:])
        weight_back = w_back[layer, 0]
        weight_in = w_in[layer, 0]
        grad_hidden = contract_last(grad_slots, weight_back)
        _, gelu_pull = jax.vjp(lambda value: jax.nn.gelu(value, approximate=False), pre_act)
        grad_pre = gelu_pull(grad_hidden)[0].astype(low)
        partial_in = contract_last(grad_pre, weight_in).astype(low)
        grad_returned = move_rows(partial_in, experts)
        back_grads[layer] = contract_first(hidden, grad_slots)
        in_grads[layer] = contract_first(arrived, grad_pre)
        grad_routed = sum_own(contract_first(dispatch, grad_returned).astype(low))
        grad_routed = grad_routed.astype(jnp.float32)
        grad_logits = (
            gate_dots - gate_probs * jnp.sum(gate_dots, axis=-1, keepdims=True)
        ).astype(low)
        router_grad = contract_first(grad_logits, routed)
        grad_routed = grad_routed + plain_dot(grad_logits, router_rows)
        grad_norm_two, gain_two, bias_two = norm_back(
            grad_routed, scaled_second, inverse_second, gain_pair[1]
        )
        grad_middle = grad_res + grad_norm_two
        grad_branch = grad_middle.astype(low)
        grad_out = jnp.stack([contract_first(grad_branch, part) for part in attended])
        grad_attended = jnp.stack([plain_dot(grad_branch, part) for part in weight_out])
        grad_attended = split_heads(grad_attended.astype(low))[0]
        grad_values = jnp.einsum(
            "gihst,gihsd->gihtd",
            probs_full.astype(low),
            grad_attended,
            preferred_element_type=jnp.float32,
        )
        grad_probs = jnp.einsum(
            "gihsd,gihtd->gihst", grad_attended, values_all, preferred_element_type=jnp.float32
        )
        grad_scores = (
            probs_full * (grad_probs - jnp.sum(probs_full * grad_probs, axis=-1, keepdims=True))
        ).astype(low)
        grad_queries = (
            jnp.einsum(
                "gihst,gihtd->gihsd", grad_scores, keys_all, preferred_element_type=jnp.float32
            )
            * scale_factor
        )
        grad_keys = (
            jnp.einsum("gihst,gihsd->gihtd", grad_scores, queries, preferred_element_type=jnp.float32)
            * scale_factor
        )
        grad_mixed = jnp.concatenate(
            [
                join_heads(grad_queries.astype(low)),
                join_heads(grad_keys.astype(low)),
                join_heads(grad_values.astype(low)),
            ],
            axis=2,
        )
        grad_normed = sum(
            contract_last(grad_mixed[part], weight_qkv[part]) for part in range(tensor_width)
        )
        grad_norm_one, gain_one, bias_one = norm_back(
            grad_normed, scaled_first, inverse_first, gain_pair[0]
        )
        grad_res = grad_middle + grad_norm_one
        grad_all = None
        grad_qkv = jnp.stack([contract_first(normed, part) for part in grad_mixed])
        qkv_grads[layer], out_grads[layer], small_grads[layer] = scatter_layer(
            jnp.concatenate([grad_qkv.astype(low), grad_out.astype(low)], axis=2),
            jnp.concatenate(
                [router_grad, jnp.stack([gain_one, gain_two, bias_one, bias_two])], axis=0
            ),
        )
    grad_tokens = drop_padding(all_tokens(grad_res.astype(low)).astype(jnp.float32))
    small_all = jnp.stack(small_grads)
    grad_router = small_all[:, :experts]
    grad_gain = small_all[:, experts : experts + 2]
    grad_bias = small_all[:, experts + 2 :]
    return (
        output,
        grad_tokens,
        grad_gain,
        grad_bias,
        jnp.stack(qkv_grads),
        jnp.stack(out_grads),
        grad_router.transpose(0, 2, 1),
        jnp.stack(in_grads)[:, None],
        jnp.stack(back_grads)[:, None],
    )


def solution(mesh):
    in_specs = (
        P(("fsdp", "expert"), None),
        P(("fsdp", "expert"), None),
        P(("fsdp", "expert"), None),
        P(None, None, "fsdp"),
        P(None, None, "fsdp"),
        P(None, "fsdp", None, "tensor"),
        P(None, "tensor", "fsdp"),
        P(None, "fsdp", None),
        P(None, ("fsdp", "expert"), None, "tensor"),
        P(None, ("fsdp", "expert"), "tensor", None),
    )
    out_specs = (
        P(("fsdp", "expert"), None),
        P(("fsdp", "expert"), None),
        P(None, None, "fsdp"),
        P(None, None, "fsdp"),
        P(None, "fsdp", None, "tensor"),
        P(None, "tensor", "fsdp"),
        P(None, "fsdp", None),
        P(None, ("fsdp", "expert"), None, "tensor"),
        P(None, ("fsdp", "expert"), "tensor", None),
    )
    return jax.shard_map(
        on_device, mesh=mesh, in_specs=in_specs, out_specs=out_specs, check_vma=False
    )
```
